512 devices in a mesh: dp: 32 (over y, x), expert: 16 (over z, core).
Axes of the slice: x: 4, y: 8, z: 8, core: 2. Of those that a mesh axis runs over, the one named last changes fastest.
Arguments:
- tokens: bfloat16 [65536, 1024], P(('dp', 'expert')), may hold values from -6 to 6
- grad_out: bfloat16 [65536, 1024], P(('dp', 'expert')), may hold values from -24 to 24
- route_ids: int32 [65536, 6], P(('dp', 'expert')), may hold values from 0 to 15, as said below
- route_slots: int32 [65536, 6], P(('dp', 'expert')), may hold values from 0 to 48, as said below
- route_probs: float32 [65536, 6], P(('dp', 'expert')), may hold values from 0.05 to 1
- w_gate: bfloat16 [16, 1024, 704], P('expert'), may hold values from -0.1875 to 0.1875
- w_up: bfloat16 [16, 1024, 704], P('expert'), may hold values from -0.1875 to 0.1875
- w_down: bfloat16 [16, 704, 1024], P('expert'), may hold values from -0.21875 to 0.21875
Outputs:
- grad_tokens: bfloat16 [65536, 1024], P(('dp', 'expert'))
- grad_down: float32 [16, 704, 1024], P('expert', None, 'dp')
The draws below stay inside these ranges and needn't reach their ends.
Inputs may be any that keep to these rules, and one draw needn't show every extreme that they name: `route_ids`: the 6 experts of a token are distinct. Among the routes of one device's 128 tokens, taken in token order and then route order, route_slots counts the earlier routes to the same expert; the value 48 marks a route dropped because that expert's 48 slots for this device are full, and kept routes to one expert from one device have distinct slots; in every device's tokens some expert is over its capacity.
All inputs are finite; a program needn't handle non-finite values.
Results may differ from the reference program's by a relative error of at most 0.024.
Values may be sent and summed in bfloat16 or wider, within the bound.
No kernel may reach another device: no remote copies, remote signals or barrier semaphores. Data moves between devices by JAX's collectives and lax.ppermute only.
A program may use at most 64 MiB of HBM per device.

```python
import math
import jax
import jax.numpy as jnp
from jax import lax

D = 1024
FF = 704
TOP = 6
TOK_DEV = 128
EXPERTS = 16
CAP = 48
TOKENS = 65536


def route_table(key):
    blocks = TOKENS // TOK_DEV
    score_key, pick_key, order_key = jax.random.split(key, 3)
    expert_iota = jnp.arange(EXPERTS, dtype=jnp.int32)
    scores = jax.random.randint(score_key, (TOKENS, EXPERTS), 0, 2 ** 20, dtype=jnp.int32) * EXPERTS + expert_iota[None, :]
    crowded = jax.random.randint(pick_key, (blocks,), 0, EXPERTS, dtype=jnp.int32)
    order = jax.random.randint(order_key, (blocks, TOK_DEV), 0, 2 ** 20, dtype=jnp.int32) * TOK_DEV + jnp.arange(TOK_DEV, dtype=jnp.int32)[None, :]
    ranking = jnp.argsort(jnp.argsort(order, axis=1), axis=1)
    favoured = (ranking <= CAP).reshape(TOKENS)
    crowded_tok = jnp.repeat(crowded, TOK_DEV)
    boost = jnp.where(favoured[:, None] & (expert_iota[None, :] == crowded_tok[:, None]), 2 ** 25, 0).astype(jnp.int32)
    top_scores, chosen = lax.top_k(scores + boost, TOP)
    chosen = chosen.astype(jnp.int32)
    hits = (chosen.reshape(blocks, TOK_DEV * TOP)[:, :, None] == expert_iota[None, None, :]).astype(jnp.int32)
    position = jnp.sum(jnp.cumsum(hits, axis=1) * hits, axis=2) - 1
    slots = jnp.minimum(position, CAP).reshape(TOKENS, TOP).astype(jnp.int32)
    return (chosen, slots)


def draw_route_ids(key, part):
    shared = route_table(key)
    return shared[0]


def draw_route_slots(key, part):
    shared = route_table(key)
    return shared[1]


def spiked(entries, stream_key, source, target, shards_of, factor):
    owner, partner = [(jnp.arange(entries.shape[dim]) // (entries.shape[dim] // shards_of)).reshape([-1 if axis == dim else 1 for axis in range(entries.ndim)]) for dim in (source, target)]
    chosen = jax.random.permutation(stream_key, shards_of)[partner]
    strong = (owner == chosen) | (owner == (partner + shards_of // 2) % shards_of)
    return jnp.where(strong, factor * entries, entries)


def block_levels(stream_key, extent, cuts, smallest, high):
    gain = 1.0
    for axis_at, shards_of in cuts:
        heights = jax.random.uniform(jax.random.fold_in(jax.random.fold_in(stream_key, 6), axis_at), (shards_of,), jnp.float32, smallest / len(cuts), high / len(cuts))
        gain = gain * jnp.repeat(jnp.exp(heights), extent[axis_at] // shards_of).reshape((-1,) + (1,) * (len(extent) - 1 - axis_at))
    return gain


def bell_draw(rng, dims, deviation, bound, pieces=(), kind=jnp.bfloat16):
    drawn = jax.random.normal(rng, dims, jnp.float32) * deviation
    if len(pieces) > 0:
        drawn = block_levels(rng, dims, pieces, -0.22, 0.18) * drawn
    return jnp.clip(drawn, min=-bound, max=bound).astype(kind)


def bell_draw_with(rng, extent, spread, most, pieces, heavy, kind=jnp.bfloat16):
    drawn = spread * jax.random.normal(rng, extent, jnp.float32)
    if pieces:
        drawn = drawn * block_levels(rng, extent, pieces, -0.22, 0.18)
    return jnp.clip(spiked(drawn, jax.random.fold_in(rng, 3), *heavy), -most, most).astype(kind)


def setup_inputs(seed: int = 0) -> dict:
    keys = jax.random.split(jax.random.key(seed), 9)
    tokens = bell_draw(keys[0], (TOKENS, D), 1.0, 6.0, ((0, 512),))
    grad_out = bell_draw_with(keys[1], (TOKENS, D), 1.0, 24.0, ((0, 512),), (0, 1, 512, 6.0))
    route_ids = draw_route_ids(jax.random.fold_in(keys[8], 71), 0)
    route_slots = draw_route_slots(jax.random.fold_in(keys[8], 71), 0)
    route_probs = jnp.clip(jnp.exp(math.log(1.0) - 2.9957323 * jax.random.uniform(keys[4], (TOKENS, TOP), jnp.float32) ** block_levels(keys[4], (TOKENS, TOP), ((0, 512),), -0.2, 0.2)), 0.05, 1.0)
    w_gate = bell_draw(keys[5], (EXPERTS, D, FF), D ** -0.5, 0.1875, ((0, 16),))
    w_up = bell_draw(keys[6], (EXPERTS, D, FF), D ** -0.5, 0.1875, ((0, 16),))
    w_down = bell_draw(keys[7], (EXPERTS, FF, D), FF ** -0.5, 0.21875, ((0, 16),))
    return dict(tokens=tokens, grad_out=grad_out, route_ids=route_ids, route_slots=route_slots, route_probs=route_probs, w_gate=w_gate, w_up=w_up, w_down=w_down)


def reference(tokens, grad_out, route_ids, route_slots, route_probs, w_gate, w_up, w_down):
    blocks = TOKENS // TOK_DEV
    buffer_rows = blocks * CAP
    block_of = jnp.arange(TOKENS, dtype=jnp.int32) // TOK_DEV
    kept = route_slots < CAP

    def per_expert(carry, inputs):
        expert, gate_weights, up_weights, down_weights = inputs
        target = jnp.where(kept & (route_ids == expert), block_of[:, None] * CAP + route_slots, buffer_rows).astype(jnp.int32)
        rows_in = jnp.zeros((buffer_rows, D), jnp.bfloat16)
        rows_grad = jnp.zeros((buffer_rows, D), jnp.bfloat16)
        weights_in = jnp.zeros((buffer_rows,), jnp.float32)
        for route_index in range(TOP):
            rows_in = rows_in.at[target[:, route_index]].set(tokens, mode="drop")
            rows_grad = rows_grad.at[target[:, route_index]].set(grad_out, mode="drop")
            weights_in = weights_in.at[target[:, route_index]].set(route_probs[:, route_index], mode="drop")
        gate_pre = jnp.dot(rows_in, gate_weights, preferred_element_type=jnp.float32)
        up_pre = jnp.dot(rows_in, up_weights, preferred_element_type=jnp.float32)
        gate_sig = jax.nn.sigmoid(gate_pre)
        activated = gate_pre * gate_sig
        hidden = (activated * up_pre).astype(jnp.bfloat16)
        scaled = (weights_in[:, None] * rows_grad.astype(jnp.float32)).astype(jnp.bfloat16)
        grad_hidden = jnp.dot(scaled, down_weights.T, preferred_element_type=jnp.float32)
        grad_gate = (grad_hidden * up_pre * gate_sig * (1.0 + gate_pre * (1.0 - gate_sig))).astype(jnp.bfloat16)
        grad_up = (grad_hidden * activated).astype(jnp.bfloat16)
        back_rows = (jnp.dot(grad_gate, gate_weights.T, preferred_element_type=jnp.float32)
                     + jnp.dot(grad_up, up_weights.T, preferred_element_type=jnp.float32)).astype(jnp.bfloat16)
        weight_grad = jnp.dot(hidden.T, scaled, preferred_element_type=jnp.float32)
        for route_index in range(TOP):
            picked = jnp.take(back_rows, target[:, route_index], axis=0, mode="fill", fill_value=0)
            carry = carry + picked.astype(jnp.float32)
        return carry, weight_grad

    expert_list = jnp.arange(EXPERTS, dtype=jnp.int32)
    start = jnp.zeros((TOKENS, D), jnp.float32)
    summed, grads = lax.scan(per_expert, start, (expert_list, w_gate, w_up, w_down))
    return summed.astype(jnp.bfloat16), grads
```

```python
import jax
import jax.numpy as jnp
from jax import lax
from jax.experimental import pallas as pl
from jax.experimental.pallas import tpu as pltpu
from jax.sharding import PartitionSpec as P

BF16 = jnp.bfloat16
F32 = jnp.float32
ROWS = 128
CAP = 48
META = 8
CHIPS = 8
VMEM = pltpu.CompilerParams(vmem_limit_bytes=40 * 1024 * 1024)
NT = (((1,), (1,)), ((), ()))
TN = (((0,), (0,)), ((), ()))


def dot(a, b, dims=(((1,), (0,)), ((), ()))):
    return lax.dot_general(a, b, dims, preferred_element_type=F32)


def call(kernel, outs, args, flops=0, scratch=()):
    moved = sum(a.size * a.dtype.itemsize for a in (*args, *outs))
    return pl.pallas_call(
        kernel,
        out_shape=outs,
        in_specs=[pl.BlockSpec(memory_space=pltpu.VMEM)] * len(args),
        out_specs=[pl.BlockSpec(memory_space=pltpu.VMEM)] * len(outs),
        scratch_shapes=list(scratch),
        compiler_params=VMEM,
        cost_estimate=pl.CostEstimate(flops=flops, bytes_accessed=moved, transcendentals=0),
    )(*args)


def shape(dims, kind=BF16):
    return jax.ShapeDtypeStruct(dims, kind)


def pack_kernel(tokens, ids, slots, probs, out):
    out[:ROWS, :] = tokens[...]
    routes = ids.shape[0]
    meta = jnp.zeros((META, out.shape[1]), F32)
    row = lax.broadcasted_iota(jnp.int32, (META, ROWS), 0)
    spare = jnp.zeros((META - routes, ROWS), F32)
    filled = [
        jnp.where(row < routes, jnp.concatenate([v.astype(F32), spare], 0), -1.0)
        for v in (ids[...], slots[...], probs[...])
    ]
    tail = jnp.zeros((META, out.shape[1] - 3 * ROWS), F32)
    out[ROWS:, :] = jnp.concatenate([*filled, tail], 1).astype(BF16)


def one_hot(meta, expert):
    ids = meta[:, :ROWS].astype(F32)
    slots = meta[:, ROWS : 2 * ROWS].astype(F32)
    probs = meta[:, 2 * ROWS : 3 * ROWS].astype(F32)
    mine = ids == expert.astype(F32)
    slot = jnp.sum(jnp.where(mine, slots + 1.0, 0.0), 0, keepdims=True) - 1.0
    prob = jnp.sum(jnp.where(mine, probs, 0.0), 0, keepdims=True)
    hit = lax.broadcasted_iota(jnp.int32, (CAP, ROWS), 0).astype(F32) == slot
    return jnp.where(hit, 1.0, 0.0), jnp.where(hit, prob, 0.0)


def select_kernel(*refs):
    toks, grads = refs[:CHIPS], refs[CHIPS : 2 * CHIPS]
    own_x, own_s, sib = refs[2 * CHIPS :]
    me = lax.axis_index("expert")
    other = me + 1 - 2 * lax.rem(me, 2)
    z = lax.div(me, 2)
    for d in range(CHIPS):
        at = lax.rem(z - d + CHIPS, CHIPS)
        meta = toks[d][ROWS:, :]
        pick, weigh = zip(one_hot(meta, me), one_hot(meta, other))
        x = dot(jnp.concatenate(pick, 0).astype(BF16), toks[d][:ROWS, :]).astype(BF16)
        s = dot(jnp.concatenate(weigh, 0).astype(BF16), grads[d][...]).astype(BF16)
        own_x[at] = x[:CAP]
        own_s[at] = s[:CAP]
        sib[0, at] = x[CAP:]
        sib[1, at] = s[CAP:]


def expert_kernel(own_x, own_s, got, w_gate, w_up, w_down, back, hidden):
    me = lax.axis_index("expert")
    core = lax.rem(me, 2)
    width = 4
    for half in range(2):
        where = core if half == 0 else 1 - core

        @pl.loop(0, CHIPS // width)
        def _(i):
            rows = pl.ds(i * width, width)
            if half == 0:
                x, s = own_x[rows], own_s[rows]
            else:
                x, s = got[0, rows], got[1, rows]
            x = x.reshape(width * CAP, -1)
            s = s.reshape(width * CAP, -1)
            gate = dot(x, w_gate[...], NT)
            up = dot(x, w_up[...], NT)
            down = dot(s, w_down[...], NT)
            sig = jax.nn.sigmoid(gate)
            act = gate * sig
            hidden[half, rows] = (act * up).astype(BF16).reshape(width, CAP, -1)
            grad_gate = (down * up * sig * (1.0 + gate * (1.0 - sig))).astype(BF16)
            grad_up = (down * act).astype(BF16)
            out = (dot(grad_gate, w_gate[...]) + dot(grad_up, w_up[...])).astype(BF16)
            for j in range(width):
                back[i * width + j, where] = out[j * CAP : (j + 1) * CAP]


def grad_kernel(own_s, got, hidden, out):
    slots = CHIPS * CAP
    parts = out.shape[0]
    own = own_s[...].reshape(slots, -1)
    theirs = got[1].reshape(slots, -1)
    for i in range(4):
        cols = slice(i * 256, (i + 1) * 256)
        total = dot(own[:, cols], hidden[0].reshape(slots, -1), TN)
        total += dot(theirs[:, cols], hidden[1].reshape(slots, -1), TN)
        out[i * parts // 4 : (i + 1) * parts // 4] = total.astype(BF16).reshape(
            parts // 4, -1, total.shape[1]
        )


def combine_kernel(ids, slots, came, out):
    spread = jnp.zeros((came.shape[0], ROWS), F32)
    row = lax.broadcasted_iota(jnp.int32, spread.shape, 0)
    for k in range(ids.shape[0]):
        slot = slots[k : k + 1, :]
        target = jnp.where(slot < CAP, ids[k : k + 1, :] * CAP + slot, -1)
        spread = jnp.where(row == target, 1.0, spread)
    out[...] = dot(spread.astype(BF16), came[...], TN).astype(BF16)


def ring(step, swap=0):
    return [
        (z * 2 + c, ((z + step) % CHIPS) * 2 + (c + swap) % 2) for z in range(CHIPS) for c in range(2)
    ]


def on_device(tokens, grad_out, route_ids, route_slots, route_probs, w_gate, w_up, w_down):
    width = tokens.shape[1]
    hidden_width = w_down.shape[1]
    parts = lax.axis_size("dp")
    ids, slots, probs = route_ids.T, route_slots.T, route_probs.T
    w_gate, w_up, w_down = w_gate[0].T, w_up[0].T, w_down[0]

    def hop(x, step, swap=0):
        return lax.ppermute(x, "expert", ring(step, swap))

    grads = {0: grad_out}
    toks = {}
    (toks[0],) = call(
        pack_kernel, [shape((ROWS + META, width))], [tokens, ids, slots, probs]
    )
    for s in (1, 2, 3):
        grads[s] = hop(grads[s - 1], 1)
        toks[-s] = hop(toks[1 - s], -1)
        toks[s] = hop(toks[s - 1], 1)
        grads[-s] = hop(grads[1 - s], -1)
    toks[4] = hop(toks[3], 1)
    grads[4] = hop(grads[-3], -1)
    order = [0, 1, 2, 3, 4, -3, -2, -1]
    rows = shape((CHIPS, CAP, width))
    own_x, own_s, sib = call(
        select_kernel,
        [rows, rows, shape((2, CHIPS, CAP, width))],
        [toks[d] for d in order] + [grads[d] for d in order],
        flops=4 * CHIPS * 2 * CAP * ROWS * width,
    )
    got = hop(sib, 0, 1)
    back, hidden = call(
        expert_kernel,
        [shape((CHIPS, 2, CAP, width)), shape((2, CHIPS, CAP, hidden_width))],
        [own_x, own_s, got, w_gate, w_up, w_down],
        flops=10 * 2 * CHIPS * CAP * width * hidden_width,
    )
    came = lax.all_to_all(
        back.reshape(2 * CHIPS, CAP, width), "expert", split_axis=0, concat_axis=0, tiled=True
    )
    (summand,) = call(
        grad_kernel,
        [shape((parts, width // parts, hidden_width))],
        [own_s, got, hidden],
        flops=2 * 2 * CHIPS * CAP * width * hidden_width,
    )
    summands = lax.all_to_all(summand, "dp", split_axis=0, concat_axis=0, tiled=True)
    grad_down = jnp.sum(summands.astype(F32), 0).T[None]
    (grad_tokens,) = call(
        combine_kernel,
        [shape((ROWS, width))],
        [ids, slots, came.reshape(2 * CHIPS * CAP, width)],
        flops=2 * 2 * CHIPS * CAP * width * ROWS,
    )
    return grad_tokens, grad_down


def solution(mesh):
    token_spec = P(("dp", "expert"), None)
    weight_spec = P("expert", None, None)
    return jax.shard_map(
        on_device,
        mesh=mesh,
        in_specs=(token_spec,) * 5 + (weight_spec,) * 3,
        out_specs=(token_spec, P("expert", None, "dp")),
        check_vma=False,
    )
```

```python
import functools

import jax
import jax.numpy as jnp
from jax import lax
from jax.experimental import pallas as pl
from jax.experimental.pallas import tpu as pltpu
from jax.sharding import PartitionSpec as P

BF16 = jnp.bfloat16
F32 = jnp.float32
ROWS = 128
CAP = 48
META = 8
CHIPS = 8
XS, YS, QUAD = 4, 8, 4
MIB = 1024 * 1024
NT = (((1,), (1,)), ((), ()))
TN = (((0,), (0,)), ((), ()))


def dot(a, b, dims=(((1,), (0,)), ((), ()))):
    return lax.dot_general(a, b, dims, preferred_element_type=F32)


def call(kernel, outs, args, flops=0, scratch=(), limit=16, after=()):
    moved = sum(a.size * a.dtype.itemsize for a in (*args, *outs))
    return pl.pallas_call(
        lambda *refs: kernel(*refs[len(after) :]),
        out_shape=outs,
        in_specs=[pl.BlockSpec(memory_space=pl.ANY)] * len(after)
        + [pl.BlockSpec(memory_space=pltpu.VMEM)] * len(args),
        out_specs=[pl.BlockSpec(memory_space=pltpu.VMEM)] * len(outs),
        scratch_shapes=list(scratch),
        compiler_params=pltpu.CompilerParams(vmem_limit_bytes=limit * MIB),
        cost_estimate=pl.CostEstimate(flops=flops, bytes_accessed=moved, transcendentals=0),
    )(*after, *args)


def shape(dims, kind=BF16):
    return jax.ShapeDtypeStruct(dims, kind)


def pack_kernel(tokens, grads, ids, slots, probs, out, out_grads, *scratch):
    sems, staged = scratch[-1], scratch[:-1]
    copies = [
        pltpu.make_async_copy(tokens, out.at[pl.ds(0, ROWS)], sems.at[3]),
        pltpu.make_async_copy(grads, out_grads, sems.at[4]),
    ]
    for i, v in enumerate((ids, slots, probs)):
        copies.append(pltpu.make_async_copy(v, staged[i], sems.at[i]))
    for c in copies:
        c.start()
    for c in copies:
        c.wait()
    width, routes = out.shape[1], ids.shape[0]
    row = lax.broadcasted_iota(jnp.int32, (META, ROWS), 0)
    spare = jnp.zeros((META - routes, ROWS), F32)
    filled = [
        jnp.where(row < routes, jnp.concatenate([v[...].astype(F32), spare], 0), -1.0)
        for v in staged
    ]
    tail = jnp.zeros((META, width - 3 * ROWS), F32)
    out[ROWS:, :] = jnp.concatenate([*filled, tail], 1).astype(BF16)


def one_hot(meta, expert):
    ids = meta[:, :ROWS].astype(F32)
    slots = meta[:, ROWS : 2 * ROWS].astype(F32)
    probs = meta[:, 2 * ROWS : 3 * ROWS].astype(F32)
    mine = ids == expert.astype(F32)
    slot = jnp.sum(jnp.where(mine, slots + 1.0, 0.0), 0, keepdims=True) - 1.0
    prob = jnp.sum(jnp.where(mine, probs, 0.0), 0, keepdims=True)
    hit = lax.broadcasted_iota(jnp.int32, (CAP, ROWS), 0).astype(F32) == slot
    return jnp.where(hit, 1.0, 0.0), jnp.where(hit, prob, 0.0)


def neighbours():
    me = lax.axis_index("expert")
    return me, me + 1 - 2 * lax.rem(me, 2)


def around(expert, step):
    return lax.rem(expert + 2 * step + 2 * CHIPS, 2 * CHIPS)


def pick(tok, grad, experts):
    meta = tok[ROWS:, :]
    hits, weights = zip(*(one_hot(meta, e) for e in experts))
    x = dot(jnp.concatenate(hits, 0).astype(BF16), tok[:ROWS, :]).astype(BF16)
    s = dot(jnp.concatenate(weights, 0).astype(BF16), grad[...]).astype(BF16)
    return x, s


def select_kernel(n, *refs):
    toks, grads, (own, sib) = refs[:n], refs[n : 2 * n], refs[2 * n :]
    me, other = neighbours()
    for d in range(n):
        x, s = pick(toks[d], grads[d], [me, other])
        for i, out in enumerate((own, sib)):
            out[0, d] = x[i * CAP : (i + 1) * CAP]
            out[1, d] = s[i * CAP : (i + 1) * CAP]


def expert_rows(own, got, w_gate, w_up, w_down, hidden):
    rows = own.shape[1] * CAP
    x = jnp.concatenate([own[0].reshape(rows, -1), got[0].reshape(rows, -1)], 0)
    s = jnp.concatenate([own[1].reshape(rows, -1), got[1].reshape(rows, -1)], 0)
    gate = dot(x, w_gate[...], NT)
    up = dot(x, w_up[...], NT)
    down = dot(s, w_down[...], NT)
    sig = jax.nn.sigmoid(gate)
    act = gate * sig
    hidden[...] = (act * up).astype(BF16)
    grad_gate = (down * up * sig * (1.0 + gate * (1.0 - sig))).astype(BF16)
    grad_up = (down * act).astype(BF16)
    return (dot(grad_gate, w_gate[...]) + dot(grad_up, w_up[...])).astype(BF16)


def first_kernel(own, got, w_gate, w_up, w_down, hidden, back, done):
    done[...] = jnp.zeros_like(done)
    back[...] = expert_rows(own, got, w_gate, w_up, w_down, hidden).reshape(back.shape)


def last_kernel(blocks, early, *refs):
    own, got, w_gate, w_up, w_down, back_early, own_early, got_early, hidden_early = refs[:9]
    back, *outs, hidden, total = refs[9:]
    me, other = neighbours()
    late = expert_rows(own, got, w_gate, w_up, w_down, hidden)
    for i, d in enumerate(early):
        back[around(me, -d)] = back_early[i]
        back[around(other, -d)] = back_early[len(early) + i]
    for i, d in enumerate(blocks):
        back[around(me, -d)] = late[i * CAP : (i + 1) * CAP]
        j = len(blocks) + i
        back[around(other, -d)] = late[j * CAP : (j + 1) * CAP]

    width = own.shape[-1]
    s = [r[1].reshape(-1, width) for r in (own_early, got_early, own, got)]
    s = jnp.concatenate(s, 0)
    h = jnp.concatenate([hidden_early[...], hidden[...]], 0)
    parts = total.shape[0]
    for i in range(4):
        cols = slice(i * width // 4, (i + 1) * width // 4)
        part = dot(s[:, cols], h, TN).astype(BF16)
        total[i * parts // 4 : (i + 1) * parts // 4] = part.reshape(parts // 4, -1, h.shape[1])
    x = dp_place()[1]
    for step, out in enumerate(outs):
        at = lax.rem(x + step, XS)
        for y in range(YS):
            out[y] = total[y * XS + at]


def dp_place():
    at = lax.axis_index("dp")
    return lax.div(at, XS), lax.rem(at, XS)


def sum_x_kernel(*refs):
    parts, outs = refs[:XS], refs[XS:]
    place = lax.rem(dp_place()[0], QUAD)
    for step, out in enumerate(outs):
        at = lax.rem(place + step, QUAD)
        for quad in range(YS // QUAD):
            out[quad] = sum(r[quad * QUAD + at].astype(F32) for r in parts).astype(BF16)


def sum_quad_kernel(*refs):
    *parts, keep, send = refs
    quad = lax.div(dp_place()[0], QUAD)
    keep[...] = sum(r[quad].astype(F32) for r in parts)
    send[...] = sum(r[1 - quad].astype(F32) for r in parts).astype(BF16)


def sum_pair_kernel(keep, got, out):
    out[...] = keep[...] + got[...].astype(F32)


def combine_kernel(ids, slots, came, out):
    spread = jnp.zeros((came.shape[0], ROWS), F32)
    row = lax.broadcasted_iota(jnp.int32, spread.shape, 0)
    for k in range(ids.shape[0]):
        slot = slots[k : k + 1, :]
        target = jnp.where(slot < CAP, ids[k : k + 1, :] * CAP + slot, -1)
        spread = jnp.where(row == target, 1.0, spread)
    out[...] = dot(spread.astype(BF16), came[...], TN).astype(BF16)


def ring(step, swap=0):
    return [
        (z * 2 + c, ((z + step) % CHIPS) * 2 + (c + swap) % 2) for z in range(CHIPS) for c in range(2)
    ]


def shift(quads, places, dx):
    return [
        (
            (q * QUAD + r) * XS + x,
            ((q + quads) % (YS // QUAD) * QUAD + (r + places) % QUAD) * XS + (x + dx) % XS,
        )
        for q in range(YS // QUAD)
        for r in range(QUAD)
        for x in range(XS)
    ]


def on_device(tokens, grad_out, route_ids, route_slots, route_probs, w_gate, w_up, w_down):
    width = tokens.shape[1]
    hidden_width = w_down.shape[1]
    ids, slots, probs = route_ids.T, route_slots.T, route_probs.T
    weights = [w_gate[0].T, w_up[0].T, w_down[0]]

    def hop(x, step, swap=0):
        return lax.ppermute(x, "expert", ring(step, swap))

    def dp_hop(x, *step):
        return lax.ppermute(x, "dp", shift(*step))

    toks, grads = {}, {}
    toks[0], grads[0] = pl.pallas_call(
        pack_kernel,
        out_shape=[shape((ROWS + META, width)), shape((ROWS, width))],
        in_specs=[pl.BlockSpec(memory_space=pl.ANY)] * 5,
        out_specs=[pl.BlockSpec(memory_space=pltpu.VMEM)] * 2,
        scratch_shapes=[
            *(pltpu.VMEM(v.shape, v.dtype) for v in (ids, slots, probs)),
            pltpu.SemaphoreType.DMA((5,)),
        ],
        compiler_params=pltpu.CompilerParams(vmem_limit_bytes=58 * MIB),
        cost_estimate=pl.CostEstimate(flops=0, bytes_accessed=tokens.size * 8, transcendentals=0),
    )(tokens, grad_out, ids, slots, probs)
    for s in (1, 2, 3):
        grads[s] = hop(grads[s - 1], 1)
        toks[-s] = hop(toks[1 - s], -1)
        toks[s] = hop(toks[s - 1], 1)
        grads[-s] = hop(grads[1 - s], -1)
    toks[4] = hop(toks[3], 1)
    grads[4] = hop(grads[-3], -1)

    def select(blocks, after=()):
        group = shape((2, len(blocks), CAP, width))
        own, sib = call(
            functools.partial(select_kernel, len(blocks)),
            [group, group],
            [toks[d] for d in blocks] + [grads[d] for d in blocks],
            flops=8 * len(blocks) * CAP * ROWS * width,
            after=after,
        )
        return own, hop(sib, 0, 1)

    early, late = [0, 1, -1, 2, -2], [3, -3, 4]
    own_a, got_a = select(early, [toks[3], grads[-3]])
    rows = 2 * len(early) * CAP
    hidden_a, back_a, done = call(
        first_kernel,
        [shape((rows, hidden_width)), shape((2 * len(early), CAP, width)), shape((8, 128), F32)],
        [own_a, got_a, *weights],
        flops=10 * rows * width * hidden_width,
        limit=32,
    )
    own_b, got_b = select(late, [done])
    rows = 2 * len(late) * CAP
    strip = width // (XS * YS)
    back, *by_x = call(
        functools.partial(last_kernel, late, early),
        [shape((2 * CHIPS, CAP, width))] + [shape((YS, strip, hidden_width))] * XS,
        [own_b, got_b, *weights, back_a, own_a, got_a, hidden_a],
        flops=10 * rows * width * hidden_width + 4 * CHIPS * CAP * width * hidden_width,
        scratch=[
            pltpu.VMEM((rows, hidden_width), BF16),
            pltpu.VMEM((XS * YS, strip, hidden_width), BF16),
        ],
        limit=32,
    )
    came = lax.all_to_all(back, "expert", split_axis=0, concat_axis=0, tiled=True)
    (grad_tokens,) = call(
        combine_kernel,
        [shape((ROWS, width))],
        [ids, slots, came.reshape(2 * CHIPS * CAP, width)],
        flops=2 * 2 * CHIPS * CAP * width * ROWS,
    )

    by_x = [by_x[0]] + [dp_hop(by_x[d], 0, 0, d) for d in range(1, XS)]
    by_y = call(sum_x_kernel, [shape((YS // QUAD, strip, hidden_width))] * QUAD, by_x)
    by_y = [by_y[0]] + [dp_hop(by_y[d], 0, d, 0) for d in range(1, QUAD)]
    one = (strip, hidden_width)
    keep, send = call(sum_quad_kernel, [shape(one, F32), shape(one)], by_y)
    (grad_down,) = call(sum_pair_kernel, [shape(one, F32)], [keep, dp_hop(send, 1, 0, 0)])
    return grad_tokens, grad_down.T[None]


def solution(mesh):
    token_spec = P(("dp", "expert"), None)
    weight_spec = P("expert", None, None)
    return jax.shard_map(
        on_device,
        mesh=mesh,
        in_specs=(token_spec,) * 5 + (weight_spec,) * 3,
        out_specs=(token_spec, P("expert", None, "dp")),
        check_vma=False,
    )
```

```python
import functools

import jax
import jax.numpy as jnp
from jax import lax
from jax.experimental import pallas as pl
from jax.experimental.pallas import tpu as pltpu
from jax.sharding import PartitionSpec as P

BF16 = jnp.bfloat16
F32 = jnp.float32
ROWS = 128
CAP = 48
META = 8
CHIPS = 8
XS, YS, PAIRS = 4, 8, 4
MIB = 1024 * 1024
NT = (((1,), (1,)), ((), ()))
TN = (((0,), (0,)), ((), ()))


def dot(a, b, dims=(((1,), (0,)), ((), ()))):
    return lax.dot_general(a, b, dims, preferred_element_type=F32)


def call(kernel, outs, args, flops=0, scratch=(), limit=16, after=(), free=False):
    moved = sum(a.size * a.dtype.itemsize for a in (*args, *outs))
    if free:
        flops, moved = 0, 0
    return pl.pallas_call(
        lambda *refs: kernel(*refs[len(after) :]),
        out_shape=outs,
        in_specs=[pl.BlockSpec(memory_space=pl.ANY)] * len(after)
        + [pl.BlockSpec(memory_space=pltpu.VMEM)] * len(args),
        out_specs=[pl.BlockSpec(memory_space=pltpu.VMEM)] * len(outs),
        scratch_shapes=list(scratch),
        compiler_params=pltpu.CompilerParams(vmem_limit_bytes=limit * MIB),
        cost_estimate=pl.CostEstimate(flops=flops, bytes_accessed=moved, transcendentals=0),
    )(*after, *args)


def shape(dims, kind=BF16):
    return jax.ShapeDtypeStruct(dims, kind)


def pack_kernel(tokens, grads, ids, slots, probs, out, out_grads, *scratch):
    sems, staged = scratch[-1], scratch[:-1]
    copies = [
        pltpu.make_async_copy(tokens, out.at[pl.ds(0, ROWS)], sems.at[3]),
        pltpu.make_async_copy(grads, out_grads, sems.at[4]),
    ]
    for i, v in enumerate((ids, slots, probs)):
        copies.append(pltpu.make_async_copy(v, staged[i], sems.at[i]))
    for c in copies:
        c.start()
    for c in copies:
        c.wait()
    width, routes = out.shape[1], ids.shape[0]
    row = lax.broadcasted_iota(jnp.int32, (META, ROWS), 0)
    spare = jnp.zeros((META - routes, ROWS), F32)
    filled = [
        jnp.where(row < routes, jnp.concatenate([v[...].astype(F32), spare], 0), -1.0)
        for v in staged
    ]
    tail = jnp.zeros((META, width - 3 * ROWS), F32)
    out[ROWS:, :] = jnp.concatenate([*filled, tail], 1).astype(BF16)


def one_hot(meta, expert):
    ids = meta[:, :ROWS].astype(F32)
    slots = meta[:, ROWS : 2 * ROWS].astype(F32)
    probs = meta[:, 2 * ROWS : 3 * ROWS].astype(F32)
    mine = ids == expert.astype(F32)
    slot = jnp.sum(jnp.where(mine, slots + 1.0, 0.0), 0, keepdims=True) - 1.0
    prob = jnp.sum(jnp.where(mine, probs, 0.0), 0, keepdims=True)
    hit = lax.broadcasted_iota(jnp.int32, (CAP, ROWS), 0).astype(F32) == slot
    return jnp.where(hit, 1.0, 0.0), jnp.where(hit, prob, 0.0)


def neighbours():
    me = lax.axis_index("expert")
    return me, me + 1 - 2 * lax.rem(me, 2)


def around(expert, step):
    return lax.rem(expert + 2 * step + 2 * CHIPS, 2 * CHIPS)


def pick(tok, grad, experts):
    meta = tok[ROWS:, :]
    hits, weights = zip(*(one_hot(meta, e) for e in experts))
    x = dot(jnp.concatenate(hits, 0).astype(BF16), tok[:ROWS, :]).astype(BF16)
    s = dot(jnp.concatenate(weights, 0).astype(BF16), grad[...]).astype(BF16)
    return x, s


def select_kernel(n, *refs):
    toks, grads, (own, sib) = refs[:n], refs[n : 2 * n], refs[2 * n :]
    me, other = neighbours()
    for d in range(n):
        x, s = pick(toks[d], grads[d], [me, other])
        for i, out in enumerate((own, sib)):
            out[0, d] = x[i * CAP : (i + 1) * CAP]
            out[1, d] = s[i * CAP : (i + 1) * CAP]


def joined(own, got, part):
    return jnp.concatenate([r[part].reshape(-1, r.shape[-1]) for r in (own, got)], 0)


def forward(own, got, w_gate, w_up):
    x = joined(own, got, 0)
    return dot(x, w_gate[...], NT), dot(x, w_up[...], NT)


def hidden_rows(gate, up):
    return (gate * jax.nn.sigmoid(gate) * up).astype(BF16)


def backward(own, got, gate, up, w_gate, w_up, w_down):
    down = dot(joined(own, got, 1), w_down[...], NT)
    sig = jax.nn.sigmoid(gate)
    grad_gate = (down * up * sig * (1.0 + gate * (1.0 - sig))).astype(BF16)
    grad_up = (down * (gate * sig)).astype(BF16)
    return (dot(grad_gate, w_gate[...]) + dot(grad_up, w_up[...])).astype(BF16)


def first_kernel(own, got, w_gate, w_up, w_down, hidden, back, done):
    done[...] = jnp.zeros_like(done)
    gate, up = forward(own, got, w_gate, w_up)
    hidden[...] = hidden_rows(gate, up)
    back[...] = backward(own, got, gate, up, w_gate, w_up, w_down).reshape(back.shape)


def weight_kernel(own, got, w_gate, w_up, own_early, got_early, hidden_early, gate, up, total, strip):
    gate[...], up[...] = forward(own, got, w_gate, w_up)
    s = jnp.concatenate([joined(own_early, got_early, 1), joined(own, got, 1)], 0)
    h = jnp.concatenate([hidden_early[...], hidden_rows(gate[...], up[...])], 0)
    parts, width = total.shape[0], s.shape[1]
    for i in range(4):
        cols = slice(i * width // 4, (i + 1) * width // 4)
        part = dot(s[:, cols], h, TN).astype(BF16)
        total[i * parts // 4 : (i + 1) * parts // 4] = part.reshape(parts // 4, -1, h.shape[1])
    take_strip(total, XS // 2, strip)


def take_strip(total, step, out):
    at = lax.rem(dp_place()[1] + step, XS)
    for y in range(YS):
        out[y] = total[y * XS + at]


def last_kernel(blocks, early, *refs):
    own, got, gate, up, w_gate, w_up, w_down, back_early, total = refs[:9]
    back, *strips = refs[9:]
    me, other = neighbours()
    late = backward(own, got, gate[...], up[...], w_gate, w_up, w_down)
    for i, d in enumerate(early):
        back[around(me, -d)] = back_early[i]
        back[around(other, -d)] = back_early[len(early) + i]
    for i, d in enumerate(blocks):
        back[around(me, -d)] = late[i * CAP : (i + 1) * CAP]
        j = len(blocks) + i
        back[around(other, -d)] = late[j * CAP : (j + 1) * CAP]
    for step, out in zip((0, 1, XS - 1), strips):
        take_strip(total, step, out)


def hold_kernel(x, out):
    pass


def hold(x, work=10**11):
    return pl.pallas_call(
        hold_kernel,
        out_shape=shape(x.shape, x.dtype),
        in_specs=[pl.BlockSpec(memory_space=pl.ANY)],
        out_specs=pl.BlockSpec(memory_space=pl.ANY),
        input_output_aliases={0: 0},
        compiler_params=pltpu.CompilerParams(vmem_limit_bytes=MIB),
        cost_estimate=pl.CostEstimate(flops=work, bytes_accessed=0, transcendentals=0),
    )(x)


def dp_place():
    at = lax.axis_index("dp")
    return lax.div(at, XS), lax.rem(at, XS)


def sum_x_kernel(*refs):
    parts, outs = refs[:XS], refs[XS:]
    pair = lax.div(dp_place()[0], 2)
    for step, out in enumerate(outs):
        at = lax.rem(pair + step, PAIRS)
        for i in range(2):
            out[i] = sum(r[2 * at + i].astype(F32) for r in parts).astype(BF16)


def sum_pairs_kernel(*refs):
    *parts, keep, send = refs
    mine = lax.rem(dp_place()[0], 2)
    keep[...] = sum(r[mine].astype(F32) for r in parts)
    send[...] = sum(r[1 - mine].astype(F32) for r in parts).astype(BF16)


def sum_last_kernel(keep, got, out):
    out[...] = keep[...] + got[...].astype(F32)


def combine_kernel(ids, slots, came, out):
    spread = jnp.zeros((came.shape[0], ROWS), F32)
    row = lax.broadcasted_iota(jnp.int32, spread.shape, 0)
    for k in range(ids.shape[0]):
        slot = slots[k : k + 1, :]
        target = jnp.where(slot < CAP, ids[k : k + 1, :] * CAP + slot, -1)
        spread = jnp.where(row == target, 1.0, spread)
    out[...] = dot(spread.astype(BF16), came[...], TN).astype(BF16)


def ring(step, swap=0):
    return [
        (z * 2 + c, ((z + step) % CHIPS) * 2 + (c + swap) % 2) for z in range(CHIPS) for c in range(2)
    ]


def shift(pairs, inside, dx):
    return [
        (
            (2 * p + i) * XS + x,
            (2 * ((p + pairs) % PAIRS) + (i + inside) % 2) * XS + (x + dx) % XS,
        )
        for p in range(PAIRS)
        for i in range(2)
        for x in range(XS)
    ]


def on_device(tokens, grad_out, route_ids, route_slots, route_probs, w_gate, w_up, w_down):
    width = tokens.shape[1]
    hidden_width = w_down.shape[1]
    ids, slots, probs = route_ids.T, route_slots.T, route_probs.T
    weights = [w_gate[0].T, w_up[0].T, w_down[0]]

    def hop(x, step, swap=0):
        return lax.ppermute(x, "expert", ring(step, swap))

    def dp_hop(x, *step):
        return lax.ppermute(x, "dp", shift(*step))

    toks, grads = {}, {}
    toks[0], grads[0] = pl.pallas_call(
        pack_kernel,
        out_shape=[shape((ROWS + META, width)), shape((ROWS, width))],
        in_specs=[pl.BlockSpec(memory_space=pl.ANY)] * 5,
        out_specs=[pl.BlockSpec(memory_space=pltpu.VMEM)] * 2,
        scratch_shapes=[
            *(pltpu.VMEM(v.shape, v.dtype) for v in (ids, slots, probs)),
            pltpu.SemaphoreType.DMA((5,)),
        ],
        compiler_params=pltpu.CompilerParams(vmem_limit_bytes=58 * MIB),
        cost_estimate=pl.CostEstimate(flops=0, bytes_accessed=tokens.size * 8, transcendentals=0),
    )(tokens, grad_out, ids, slots, probs)
    for s in (1, 2, 3):
        grads[s] = hop(grads[s - 1], 1)
        toks[-s] = hop(toks[1 - s], -1)
        toks[s] = hop(toks[s - 1], 1)
        grads[-s] = hop(grads[1 - s], -1)
    toks[4] = hop(toks[3], 1)
    grads[4] = hop(grads[-3], -1)

    toks[-3] = hold(toks[-3], 10**10)

    grads[3] = hold(grads[3], 10**10)

    def select(blocks, after=()):
        group = shape((2, len(blocks), CAP, width))
        own, sib = call(
            functools.partial(select_kernel, len(blocks)),
            [group, group],
            [toks[d] for d in blocks] + [grads[d] for d in blocks],
            flops=8 * len(blocks) * CAP * ROWS * width,
            after=after,
            free=True,
        )
        return own, hop(sib, 0, 1)

    early, late = [0, 1, -1, 2, -2], [3, -3, 4]
    own_a, got_a = select(early, [toks[3], grads[-3]])
    rows = 2 * len(early) * CAP
    hidden_a, back_a, done = call(
        first_kernel,
        [shape((rows, hidden_width)), shape((2 * len(early), CAP, width)), shape((8, 128), F32)],
        [own_a, got_a, *weights],
        flops=10 * rows * width * hidden_width,
        limit=32,
        free=True,
    )
    own_b, got_b = select(late, [done])
    rows = 2 * len(late) * CAP
    cols = width // (XS * YS)
    strip = shape((YS, cols, hidden_width))
    wide = shape((rows, hidden_width), F32)
    gate, up, total, strip2 = call(
        weight_kernel,
        [wide, wide, shape((XS * YS, cols, hidden_width)), strip],
        [own_b, got_b, *weights[:2], own_a, got_a, hidden_a],
        flops=4 * rows * width * hidden_width + 4 * CHIPS * CAP * width * hidden_width,
        limit=24,
    )
    strip2 = hold(dp_hop(strip2, 0, 0, 2))
    back, strip0, strip1, strip3 = call(
        functools.partial(last_kernel, late, early),
        [shape((2 * CHIPS, CAP, width))] + [strip] * 3,
        [own_b, got_b, gate, up, *weights, back_a, total],
        flops=6 * rows * width * hidden_width,
        limit=32,
    )
    came = lax.all_to_all(back, "expert", split_axis=0, concat_axis=0, tiled=True)
    (grad_tokens,) = call(
        combine_kernel,
        [shape((ROWS, width))],
        [ids, slots, came.reshape(2 * CHIPS * CAP, width)],
        flops=2 * 2 * CHIPS * CAP * width * ROWS,
    )

    by_x = [strip0, dp_hop(strip1, 0, 0, 1), strip2, dp_hop(strip3, 0, 0, 3)]
    by_y = call(sum_x_kernel, [shape((2, cols, hidden_width))] * PAIRS, by_x)
    by_y = [by_y[0]] + [dp_hop(by_y[d], d, 0, 0) for d in range(1, PAIRS)]
    one = (cols, hidden_width)
    keep, send = call(sum_pairs_kernel, [shape(one, F32), shape(one)], by_y)
    (grad_down,) = call(sum_last_kernel, [shape(one, F32)], [keep, dp_hop(send, 0, 1, 0)])
    return grad_tokens, grad_down.T[None]


def solution(mesh):
    token_spec = P(("dp", "expert"), None)
    weight_spec = P("expert", None, None)
    return jax.shard_map(
        on_device,
        mesh=mesh,
        in_specs=(token_spec,) * 5 + (weight_spec,) * 3,
        out_specs=(token_spec, P("expert", None, "dp")),
        check_vma=False,
    )
```

```python
import functools

import jax
import jax.numpy as jnp
from jax import lax
from jax.experimental import pallas as pl
from jax.experimental.pallas import tpu as pltpu
from jax.sharding import PartitionSpec as P

BF16 = jnp.bfloat16
F32 = jnp.float32
ROWS = 128
CAP = 48
META = 8
CHIPS = 8
XS, YS, QUAD = 4, 8, 4
MIB = 1024 * 1024
NT = (((1,), (1,)), ((), ()))
TN = (((0,), (0,)), ((), ()))


def dot(a, b, dims=(((1,), (0,)), ((), ()))):
    return lax.dot_general(a, b, dims, preferred_element_type=F32)


def call(kernel, outs, args, flops=0, scratch=(), limit=16, after=(), free=False):
    moved = sum(a.size * a.dtype.itemsize for a in (*args, *outs))
    if free:
        flops, moved = 0, 0
    return pl.pallas_call(
        lambda *refs: kernel(*refs[len(after) :]),
        out_shape=outs,
        in_specs=[pl.BlockSpec(memory_space=pl.ANY)] * len(after)
        + [pl.BlockSpec(memory_space=pltpu.VMEM)] * len(args),
        out_specs=[pl.BlockSpec(memory_space=pltpu.VMEM)] * len(outs),
        scratch_shapes=list(scratch),
        compiler_params=pltpu.CompilerParams(vmem_limit_bytes=limit * MIB),
        cost_estimate=pl.CostEstimate(flops=flops, bytes_accessed=moved, transcendentals=0),
    )(*after, *args)


def shape(dims, kind=BF16):
    return jax.ShapeDtypeStruct(dims, kind)


def pack_kernel(tokens, grads, ids, slots, probs, out, out_grads, *scratch):
    sems, staged = scratch[-1], scratch[:-1]
    copies = [
        pltpu.make_async_copy(tokens, out.at[pl.ds(0, ROWS)], sems.at[3]),
        pltpu.make_async_copy(grads, out_grads, sems.at[4]),
    ]
    for i, v in enumerate((ids, slots, probs)):
        copies.append(pltpu.make_async_copy(v, staged[i], sems.at[i]))
    for c in copies:
        c.start()
    for c in copies:
        c.wait()
    width, routes = out.shape[1], ids.shape[0]
    row = lax.broadcasted_iota(jnp.int32, (META, ROWS), 0)
    spare = jnp.zeros((META - routes, ROWS), F32)
    filled = [
        jnp.where(row < routes, jnp.concatenate([v[...].astype(F32), spare], 0), -1.0)
        for v in staged
    ]
    tail = jnp.zeros((META, width - 3 * ROWS), F32)
    out[ROWS:, :] = jnp.concatenate([*filled, tail], 1).astype(BF16)


def one_hot(meta, expert):
    ids = meta[:, :ROWS].astype(F32)
    slots = meta[:, ROWS : 2 * ROWS].astype(F32)
    probs = meta[:, 2 * ROWS : 3 * ROWS].astype(F32)
    mine = ids == expert.astype(F32)
    slot = jnp.sum(jnp.where(mine, slots + 1.0, 0.0), 0, keepdims=True) - 1.0
    prob = jnp.sum(jnp.where(mine, probs, 0.0), 0, keepdims=True)
    hit = lax.broadcasted_iota(jnp.int32, (CAP, ROWS), 0).astype(F32) == slot
    return jnp.where(hit, 1.0, 0.0), jnp.where(hit, prob, 0.0)


def neighbours():
    me = lax.axis_index("expert")
    return me, me + 1 - 2 * lax.rem(me, 2)


def around(expert, step):
    return lax.rem(expert + 2 * step + 2 * CHIPS, 2 * CHIPS)


def pick(tok, grad, experts):
    meta = tok[ROWS:, :]
    hits, weights = zip(*(one_hot(meta, e) for e in experts))
    x = dot(jnp.concatenate(hits, 0).astype(BF16), tok[:ROWS, :]).astype(BF16)
    s = dot(jnp.concatenate(weights, 0).astype(BF16), grad[...]).astype(BF16)
    return x, s


def select_kernel(n, which, *refs):
    toks, grads, outs = refs[:n], refs[n : 2 * n], refs[2 * n :]
    experts = neighbours()
    for d in range(n):
        x, s = pick(toks[d], grads[d], [experts[i] for i in which])
        for i, out in enumerate(outs):
            out[0, d] = x[i * CAP : (i + 1) * CAP]
            out[1, d] = s[i * CAP : (i + 1) * CAP]


def own_kernel(n, *refs):
    blocks, weights, (own, *outs) = refs[: 2 * n], refs[2 * n : 2 * n + 3], refs[2 * n + 3 :]
    select_kernel(n, [0], *blocks, own)
    early_kernel(own, *weights, *outs)


def joined(groups, part):
    return jnp.concatenate([g[part].reshape(-1, g.shape[-1]) for g in groups], 0)


def forward(groups, w_gate, w_up):
    x = joined(groups, 0)
    return dot(x, w_gate[...], NT), dot(x, w_up[...], NT)


def hidden_rows(gate, up):
    return (gate * jax.nn.sigmoid(gate) * up).astype(BF16)


def backward(groups, gate, up, w_gate, w_up, w_down):
    down = dot(joined(groups, 1), w_down[...], NT)
    sig = jax.nn.sigmoid(gate)
    grad_gate = (down * up * sig * (1.0 + gate * (1.0 - sig))).astype(BF16)
    grad_up = (down * (gate * sig)).astype(BF16)
    return (dot(grad_gate, w_gate[...]) + dot(grad_up, w_up[...])).astype(BF16)


def early_kernel(group, w_gate, w_up, w_down, hidden, back, done):
    done[...] = jnp.zeros_like(done)
    gate, up = forward([group], w_gate, w_up)
    hidden[...] = hidden_rows(gate, up)
    back[...] = backward([group], gate, up, w_gate, w_up, w_down).reshape(back.shape)


def weight_kernel(own, got, w_gate, w_up, own_a, got_a, hidden_a, hidden_x, gate, up, total, strip):
    gate[...], up[...] = forward([own, got], w_gate, w_up)
    s = joined([own_a, got_a, own, got], 1)
    h = jnp.concatenate([hidden_a[...], hidden_x[...], hidden_rows(gate[...], up[...])], 0)
    parts, width = total.shape[0], s.shape[1]
    for i in range(4):
        cols = slice(i * width // 4, (i + 1) * width // 4)
        part = dot(s[:, cols], h, TN).astype(BF16)
        total[i * parts // 4 : (i + 1) * parts // 4] = part.reshape(parts // 4, -1, h.shape[1])
    take_strip(total, XS // 2, strip)


def take_strip(total, step, out):
    at = lax.rem(dp_place()[1] + step, XS)
    for y in range(YS):
        out[y] = total[y * XS + at]


def last_kernel(blocks, early, *refs):
    own, got, gate, up, w_gate, w_up, w_down, back_a, back_x, total = refs[:10]
    back, *strips = refs[10:]
    me, other = neighbours()
    late = backward([own, got], gate[...], up[...], w_gate, w_up, w_down)
    for i, d in enumerate(early):
        back[around(me, -d)] = back_a[i]
        back[around(other, -d)] = back_x[i]
    for i, d in enumerate(blocks):
        back[around(me, -d)] = late[i * CAP : (i + 1) * CAP]
        j = len(blocks) + i
        back[around(other, -d)] = late[j * CAP : (j + 1) * CAP]
    for step, out in zip((0, 1, XS - 1), strips):
        take_strip(total, step, out)


def hold_kernel(x, out):
    pass


def hold(x, work=10**11):
    return pl.pallas_call(
        hold_kernel,
        out_shape=shape(x.shape, x.dtype),
        in_specs=[pl.BlockSpec(memory_space=pl.ANY)],
        out_specs=pl.BlockSpec(memory_space=pl.ANY),
        input_output_aliases={0: 0},
        compiler_params=pltpu.CompilerParams(vmem_limit_bytes=MIB),
        cost_estimate=pl.CostEstimate(flops=work, bytes_accessed=0, transcendentals=0),
    )(x)


def dp_place():
    at = lax.axis_index("dp")
    return lax.div(at, XS), lax.rem(at, XS)


def sum_x_kernel(*refs):
    parts, outs = refs[:XS], refs[XS:]
    place = lax.rem(dp_place()[0], QUAD)
    for step, out in enumerate(outs):
        at = lax.rem(place + step, QUAD)
        for quad in range(YS // QUAD):
            out[quad] = sum(r[quad * QUAD + at].astype(F32) for r in parts).astype(BF16)


def sum_quad_kernel(*refs):
    *parts, keep, send = refs
    quad = lax.div(dp_place()[0], QUAD)
    keep[...] = sum(r[quad].astype(F32) for r in parts)
    send[...] = sum(r[1 - quad].astype(F32) for r in parts).astype(BF16)


def sum_last_kernel(keep, got, out):
    out[...] = keep[...] + got[...].astype(F32)


def combine_kernel(ids, slots, came, out):
    spread = jnp.zeros((came.shape[0], ROWS), F32)
    row = lax.broadcasted_iota(jnp.int32, spread.shape, 0)
    for k in range(ids.shape[0]):
        slot = slots[k : k + 1, :]
        target = jnp.where(slot < CAP, ids[k : k + 1, :] * CAP + slot, -1)
        spread = jnp.where(row == target, 1.0, spread)
    out[...] = dot(spread.astype(BF16), came[...], TN).astype(BF16)


def ring(step, swap=0):
    return [
        (z * 2 + c, ((z + step) % CHIPS) * 2 + (c + swap) % 2) for z in range(CHIPS) for c in range(2)
    ]


def shift(quads, places, dx):
    return [
        (
            (q * QUAD + r) * XS + x,
            ((q + quads) % (YS // QUAD) * QUAD + (r + places) % QUAD) * XS + (x + dx) % XS,
        )
        for q in range(YS // QUAD)
        for r in range(QUAD)
        for x in range(XS)
    ]


def on_device(tokens, grad_out, route_ids, route_slots, route_probs, w_gate, w_up, w_down):
    width = tokens.shape[1]
    hidden_width = w_down.shape[1]
    ids, slots, probs = route_ids.T, route_slots.T, route_probs.T
    weights = [w_gate[0].T, w_up[0].T, w_down[0]]

    def hop(x, step, swap=0):
        return lax.ppermute(x, "expert", ring(step, swap))

    def dp_hop(x, *step):
        return lax.ppermute(x, "dp", shift(*step))

    toks, grads = {}, {}
    toks[0], grads[0] = pl.pallas_call(
        pack_kernel,
        out_shape=[shape((ROWS + META, width)), shape((ROWS, width))],
        in_specs=[pl.BlockSpec(memory_space=pl.ANY)] * 5,
        out_specs=[pl.BlockSpec(memory_space=pltpu.VMEM)] * 2,
        scratch_shapes=[
            *(pltpu.VMEM(v.shape, v.dtype) for v in (ids, slots, probs)),
            pltpu.SemaphoreType.DMA((5,)),
        ],
        compiler_params=pltpu.CompilerParams(vmem_limit_bytes=58 * MIB),
        cost_estimate=pl.CostEstimate(flops=0, bytes_accessed=tokens.size * 8, transcendentals=0),
    )(tokens, grad_out, ids, slots, probs)
    for s in (1, 2, 3):
        grads[s] = hop(grads[s - 1], 1)
        toks[-s] = hop(toks[1 - s], -1)
        toks[s] = hop(toks[s - 1], 1)
        grads[-s] = hop(grads[1 - s], -1)
    toks[4] = hop(toks[3], 1)
    grads[4] = hop(grads[-3], -1)

    def blocks(which):
        return [toks[d] for d in which] + [grads[d] for d in which]

    def select(which, experts, after):
        return call(
            functools.partial(select_kernel, len(which), experts),
            [shape((2, len(which), CAP, width))] * len(experts),
            blocks(which),
            flops=4 * len(experts) * len(which) * CAP * ROWS * width,
            after=after,
            free=True,
        )

    early, late = [0, 1, -1, 2, -2], [3, -3, 4]
    rows = len(early) * CAP
    group = shape((2, len(early), CAP, width))
    results = [
        shape((rows, hidden_width)),
        shape((len(early), CAP, width)),
        shape((8, 128), F32),
    ]
    own_a, hidden_a, back_a, done = call(
        functools.partial(own_kernel, len(early)),
        [group, *results],
        [*blocks(early), *weights],
        flops=10 * rows * width * hidden_width,
        limit=32,
        after=[toks[3], grads[-3]],
        free=True,
    )
    (sib_a,) = select(early, [1], [done, toks[4], grads[4]])
    got_a = hop(sib_a, 0, 1)
    hidden_x, back_x, _ = call(
        early_kernel,
        results,
        [got_a, *weights],
        flops=10 * rows * width * hidden_width,
        limit=32,
    )
    toks[-3] = hold(toks[-3], 10**10)
    grads[3] = hold(grads[3], 10**10)
    own_b, sib_b = select(late, [0, 1], [done])
    got_b = hop(sib_b, 0, 1)
    rows = 2 * len(late) * CAP
    cols = width // (XS * YS)
    strip = shape((YS, cols, hidden_width))
    wide = shape((rows, hidden_width), F32)
    gate, up, total, strip2 = call(
        weight_kernel,
        [wide, wide, shape((XS * YS, cols, hidden_width)), strip],
        [own_b, got_b, *weights[:2], own_a, got_a, hidden_a, hidden_x],
        flops=4 * rows * width * hidden_width + 4 * CHIPS * CAP * width * hidden_width,
        limit=24,
    )
    strip2 = hold(dp_hop(strip2, 0, 0, 2))
    back, strip0, strip1, strip3 = call(
        functools.partial(last_kernel, late, early),
        [shape((2 * CHIPS, CAP, width))] + [strip] * 3,
        [own_b, got_b, gate, up, *weights, back_a, back_x, total],
        flops=6 * rows * width * hidden_width,
        limit=32,
    )
    came = lax.all_to_all(back, "expert", split_axis=0, concat_axis=0, tiled=True)
    (grad_tokens,) = call(
        combine_kernel,
        [shape((ROWS, width))],
        [ids, slots, came.reshape(2 * CHIPS * CAP, width)],
        flops=2 * 2 * CHIPS * CAP * width * ROWS,
    )

    by_x = [strip0, dp_hop(strip1, 0, 0, 1), strip2, dp_hop(strip3, 0, 0, 3)]
    by_y = call(sum_x_kernel, [shape((YS // QUAD, cols, hidden_width))] * QUAD, by_x)
    by_y = [by_y[0]] + [dp_hop(by_y[d], 0, d, 0) for d in range(1, QUAD)]
    one = (cols, hidden_width)
    keep, send = call(sum_quad_kernel, [shape(one, F32), shape(one)], by_y)
    (grad_down,) = call(sum_last_kernel, [shape(one, F32)], [keep, dp_hop(send, 1, 0, 0)])
    return grad_tokens, grad_down.T[None]


def solution(mesh):
    token_spec = P(("dp", "expert"), None)
    weight_spec = P("expert", None, None)
    return jax.shard_map(
        on_device,
        mesh=mesh,
        in_specs=(token_spec,) * 5 + (weight_spec,) * 3,
        out_specs=(token_spec, P("expert", None, "dp")),
        check_vma=False,
    )
```

```python
import functools

import jax
import jax.numpy as jnp
from jax import lax
from jax.experimental import pallas as pl
from jax.experimental.pallas import tpu as pltpu
from jax.sharding import PartitionSpec as P

BF16 = jnp.bfloat16
F32 = jnp.float32
ROWS = 128
CAP = 48
META = 8
CHIPS = 8
XS, YS, QUAD = 4, 8, 4
MIB = 1024 * 1024
NT = (((1,), (1,)), ((), ()))
TN = (((0,), (0,)), ((), ()))


def dot(a, b, dims=(((1,), (0,)), ((), ()))):
    return lax.dot_general(a, b, dims, preferred_element_type=F32)


def call(kernel, outs, args, flops=0, scratch=(), limit=16, after=(), free=False):
    moved = sum(a.size * a.dtype.itemsize for a in (*args, *outs))
    if free:
        flops, moved = 0, 0
    return pl.pallas_call(
        lambda *refs: kernel(*refs[len(after) :]),
        out_shape=outs,
        in_specs=[pl.BlockSpec(memory_space=pl.ANY)] * len(after)
        + [pl.BlockSpec(memory_space=pltpu.VMEM)] * len(args),
        out_specs=[pl.BlockSpec(memory_space=pltpu.VMEM)] * len(outs),
        scratch_shapes=list(scratch),
        compiler_params=pltpu.CompilerParams(vmem_limit_bytes=limit * MIB),
        cost_estimate=pl.CostEstimate(flops=flops, bytes_accessed=moved, transcendentals=0),
    )(*after, *args)


def shape(dims, kind=BF16):
    return jax.ShapeDtypeStruct(dims, kind)


def pack_kernel(tokens, grads, ids, slots, probs, out, out_grads, *scratch):
    sems, staged = scratch[-1], scratch[:-1]
    copies = [
        pltpu.make_async_copy(tokens, out.at[pl.ds(0, ROWS)], sems.at[3]),
        pltpu.make_async_copy(grads, out_grads, sems.at[4]),
    ]
    for i, v in enumerate((ids, slots, probs)):
        copies.append(pltpu.make_async_copy(v, staged[i], sems.at[i]))
    for c in copies:
        c.start()
    for c in copies:
        c.wait()
    width, routes = out.shape[1], ids.shape[0]
    row = lax.broadcasted_iota(jnp.int32, (META, ROWS), 0)
    spare = jnp.zeros((META - routes, ROWS), F32)
    filled = [
        jnp.where(row < routes, jnp.concatenate([v[...].astype(F32), spare], 0), -1.0)
        for v in staged
    ]
    tail = jnp.zeros((META, width - 3 * ROWS), F32)
    out[ROWS:, :] = jnp.concatenate([*filled, tail], 1).astype(BF16)


def one_hot(meta, expert):
    ids = meta[:, :ROWS].astype(F32)
    slots = meta[:, ROWS : 2 * ROWS].astype(F32)
    probs = meta[:, 2 * ROWS : 3 * ROWS].astype(F32)
    mine = ids == expert.astype(F32)
    slot = jnp.sum(jnp.where(mine, slots + 1.0, 0.0), 0, keepdims=True) - 1.0
    prob = jnp.sum(jnp.where(mine, probs, 0.0), 0, keepdims=True)
    hit = lax.broadcasted_iota(jnp.int32, (CAP, ROWS), 0).astype(F32) == slot
    return jnp.where(hit, 1.0, 0.0), jnp.where(hit, prob, 0.0)


def neighbours():
    me = lax.axis_index("expert")
    return me, me + 1 - 2 * lax.rem(me, 2)


def around(expert, step):
    return lax.rem(expert + 2 * step + 2 * CHIPS, 2 * CHIPS)


def pick(tok, grad, experts):
    meta = tok[ROWS:, :]
    hits, weights = zip(*(one_hot(meta, e) for e in experts))
    x = dot(jnp.concatenate(hits, 0).astype(BF16), tok[:ROWS, :]).astype(BF16)
    s = dot(jnp.concatenate(weights, 0).astype(BF16), grad[...]).astype(BF16)
    return x, s


def select_kernel(n, which, *refs):
    toks, grads, outs = refs[:n], refs[n : 2 * n], refs[2 * n :]
    experts = neighbours()
    for d in range(n):
        x, s = pick(toks[d], grads[d], [experts[i] for i in which])
        for i, out in enumerate(outs):
            out[0, d] = x[i * CAP : (i + 1) * CAP]
            out[1, d] = s[i * CAP : (i + 1) * CAP]


def own_kernel(n, *refs):
    blocks, weights, (own, *outs) = refs[: 2 * n], refs[2 * n : 2 * n + 3], refs[2 * n + 3 :]
    select_kernel(n, [0], *blocks, own)
    early_kernel(own, *weights, *outs)


def joined(groups, part):
    return jnp.concatenate([g[part].reshape(-1, g.shape[-1]) for g in groups], 0)


def forward(groups, w_gate, w_up):
    x = joined(groups, 0)
    return dot(x, w_gate[...], NT), dot(x, w_up[...], NT)


def hidden_rows(gate, up):
    return (gate * jax.nn.sigmoid(gate) * up).astype(BF16)


def backward(groups, gate, up, w_gate, w_up, w_down):
    down = dot(joined(groups, 1), w_down[...], NT)
    sig = jax.nn.sigmoid(gate)
    grad_gate = (down * up * sig * (1.0 + gate * (1.0 - sig))).astype(BF16)
    grad_up = (down * (gate * sig)).astype(BF16)
    return (dot(grad_gate, w_gate[...]) + dot(grad_up, w_up[...])).astype(BF16)


def early_kernel(group, w_gate, w_up, w_down, hidden, back, done):
    done[...] = jnp.zeros_like(done)
    gate, up = forward([group], w_gate, w_up)
    hidden[...] = hidden_rows(gate, up)
    back[...] = backward([group], gate, up, w_gate, w_up, w_down).reshape(back.shape)


def weight_kernel(own, got, w_gate, w_up, own_a, got_a, hidden_a, hidden_x, gate, up, total, strip):
    gate[...], up[...] = forward([own, got], w_gate, w_up)
    s = joined([own_a, got_a, own, got], 1)
    h = jnp.concatenate([hidden_a[...], hidden_x[...], hidden_rows(gate[...], up[...])], 0)
    parts, width = total.shape[0], s.shape[1]
    for i in range(4):
        cols = slice(i * width // 4, (i + 1) * width // 4)
        part = dot(s[:, cols], h, TN).astype(BF16)
        total[i * parts // 4 : (i + 1) * parts // 4] = part.reshape(parts // 4, -1, h.shape[1])
    take_strip(total, XS // 2, strip)


def take_strip(total, step, out):
    at = lax.bitwise_xor(dp_place()[1], step)
    for y in range(YS):
        out[y] = total[y * XS + at]


def last_kernel(blocks, early, *refs):
    own, got, gate, up, w_gate, w_up, w_down, back_a, back_x, total = refs[:10]
    back, *strips = refs[10:]
    me, other = neighbours()
    late = backward([own, got], gate[...], up[...], w_gate, w_up, w_down)
    for i, d in enumerate(early):
        back[around(me, -d)] = back_a[i]
        back[around(other, -d)] = back_x[i]
    for i, d in enumerate(blocks):
        back[around(me, -d)] = late[i * CAP : (i + 1) * CAP]
        j = len(blocks) + i
        back[around(other, -d)] = late[j * CAP : (j + 1) * CAP]
    for step, out in zip((0, 1, XS - 1), strips):
        take_strip(total, step, out)


def hold_kernel(x, out):
    pass


def hold(x, work=10**11):
    return pl.pallas_call(
        hold_kernel,
        out_shape=shape(x.shape, x.dtype),
        in_specs=[pl.BlockSpec(memory_space=pl.ANY)],
        out_specs=pl.BlockSpec(memory_space=pl.ANY),
        input_output_aliases={0: 0},
        compiler_params=pltpu.CompilerParams(vmem_limit_bytes=MIB),
        cost_estimate=pl.CostEstimate(flops=work, bytes_accessed=0, transcendentals=0),
    )(x)


def dp_place():
    at = lax.axis_index("dp")
    return lax.div(at, XS), lax.rem(at, XS)


def sum_x_kernel(*refs):
    parts, outs = refs[:XS], refs[XS:]
    place = lax.rem(dp_place()[0], QUAD)
    for step, out in enumerate(outs):
        at = lax.rem(place + step, QUAD)
        for quad in range(YS // QUAD):
            out[quad] = sum(r[quad * QUAD + at].astype(F32) for r in parts).astype(BF16)


def sum_quad_kernel(*refs):
    *parts, keep, send = refs
    quad = lax.div(dp_place()[0], QUAD)
    keep[...] = sum(r[quad].astype(F32) for r in parts)
    send[...] = sum(r[1 - quad].astype(F32) for r in parts).astype(BF16)


def sum_last_kernel(keep, got, out):
    out[...] = keep[...] + got[...].astype(F32)


def combine_kernel(ids, slots, came, out, done):
    done[...] = jnp.zeros_like(done)
    spread = jnp.zeros((came.shape[0], ROWS), F32)
    row = lax.broadcasted_iota(jnp.int32, spread.shape, 0)
    for k in range(ids.shape[0]):
        slot = slots[k : k + 1, :]
        target = jnp.where(slot < CAP, ids[k : k + 1, :] * CAP + slot, -1)
        spread = jnp.where(row == target, 1.0, spread)
    out[...] = dot(spread.astype(BF16), came[...], TN).astype(BF16)


def ring(step, swap=0):
    return [
        (z * 2 + c, ((z + step) % CHIPS) * 2 + (c + swap) % 2) for z in range(CHIPS) for c in range(2)
    ]


def along_x(bits):
    return [(y * XS + x, y * XS + (x ^ bits)) for y in range(YS) for x in range(XS)]


def along_y(quads, places):
    return [
        ((q * QUAD + r) * XS + x, ((q + quads) % (YS // QUAD) * QUAD + (r + places) % QUAD) * XS + x)
        for q in range(YS // QUAD)
        for r in range(QUAD)
        for x in range(XS)
    ]


def on_device(tokens, grad_out, route_ids, route_slots, route_probs, w_gate, w_up, w_down):
    width = tokens.shape[1]
    hidden_width = w_down.shape[1]
    ids, slots, probs = route_ids.T, route_slots.T, route_probs.T
    weights = [w_gate[0].T, w_up[0].T, w_down[0]]

    def hop(x, step, swap=0):
        return lax.ppermute(x, "expert", ring(step, swap))

    def dp_hop(x, pairs):
        return lax.ppermute(x, "dp", pairs)

    toks, grads = {}, {}
    toks[0], grads[0] = pl.pallas_call(
        pack_kernel,
        out_shape=[shape((ROWS + META, width)), shape((ROWS, width))],
        in_specs=[pl.BlockSpec(memory_space=pl.ANY)] * 5,
        out_specs=[pl.BlockSpec(memory_space=pltpu.VMEM)] * 2,
        scratch_shapes=[
            *(pltpu.VMEM(v.shape, v.dtype) for v in (ids, slots, probs)),
            pltpu.SemaphoreType.DMA((5,)),
        ],
        compiler_params=pltpu.CompilerParams(vmem_limit_bytes=58 * MIB),
        cost_estimate=pl.CostEstimate(flops=0, bytes_accessed=tokens.size * 8, transcendentals=0),
    )(tokens, grad_out, ids, slots, probs)
    for s in (1, 2, 3):
        grads[s] = hop(grads[s - 1], 1)
        toks[-s] = hop(toks[1 - s], -1)
        toks[s] = hop(toks[s - 1], 1)
        grads[-s] = hop(grads[1 - s], -1)
    toks[4] = hop(toks[3], 1)
    grads[4] = hop(grads[-3], -1)

    def blocks(which):
        return [toks[d] for d in which] + [grads[d] for d in which]

    def select(which, experts, after):
        return call(
            functools.partial(select_kernel, len(which), experts),
            [shape((2, len(which), CAP, width))] * len(experts),
            blocks(which),
            flops=4 * len(experts) * len(which) * CAP * ROWS * width,
            after=after,
            free=True,
        )

    early, late = [0, 1, -1, 2, -2], [3, -3, 4]
    rows = len(early) * CAP
    group = shape((2, len(early), CAP, width))
    results = [
        shape((rows, hidden_width)),
        shape((len(early), CAP, width)),
        shape((8, 128), F32),
    ]
    own_a, hidden_a, back_a, done = call(
        functools.partial(own_kernel, len(early)),
        [group, *results],
        [*blocks(early), *weights],
        flops=10 * rows * width * hidden_width,
        limit=32,
        after=[toks[3], grads[-3]],
        free=True,
    )
    (sib_a,) = select(early, [1], [done, toks[4], grads[4]])
    got_a = hop(sib_a, 0, 1)
    hidden_x, back_x, _ = call(
        early_kernel,
        results,
        [got_a, *weights],
        flops=10 * rows * width * hidden_width,
        limit=32,
    )
    toks[-3] = hold(toks[-3], 10**10)
    grads[3] = hold(grads[3], 10**10)
    own_b, sib_b = select(late, [0, 1], [done])
    got_b = hop(sib_b, 0, 1)
    rows = 2 * len(late) * CAP
    cols = width // (XS * YS)
    strip = shape((YS, cols, hidden_width))
    wide = shape((rows, hidden_width), F32)
    gate, up, total, strip2 = call(
        weight_kernel,
        [wide, wide, shape((XS * YS, cols, hidden_width)), strip],
        [own_b, got_b, *weights[:2], own_a, got_a, hidden_a, hidden_x],
        flops=4 * rows * width * hidden_width + 4 * CHIPS * CAP * width * hidden_width,
        limit=24,
    )
    strip2 = hold(dp_hop(strip2, along_x(2)))
    back, strip0, strip1, strip3 = call(
        functools.partial(last_kernel, late, early),
        [shape((2 * CHIPS, CAP, width))] + [strip] * 3,
        [own_b, got_b, gate, up, *weights, back_a, back_x, total],
        flops=6 * rows * width * hidden_width,
        limit=32,
    )
    came = lax.all_to_all(back, "expert", split_axis=0, concat_axis=0, tiled=True)
    grad_tokens, combined = call(
        combine_kernel,
        [shape((ROWS, width)), shape((8, 128), F32)],
        [ids, slots, came.reshape(2 * CHIPS * CAP, width)],
        flops=2 * 2 * CHIPS * CAP * width * ROWS,
    )

    by_x = [strip0, dp_hop(strip1, along_x(1)), strip2, dp_hop(strip3, along_x(3))]
    by_y = call(sum_x_kernel, [shape((YS // QUAD, cols, hidden_width))] * QUAD, by_x)
    by_y = [by_y[0]] + [dp_hop(by_y[d], along_y(0, d)) for d in range(1, QUAD)]
    one = (cols, hidden_width)
    keep, send = call(sum_quad_kernel, [shape(one, F32), shape(one)], by_y)
    (grad_down,) = call(
        sum_last_kernel,
        [shape(one, F32)],
        [keep, dp_hop(send, along_y(1, 0))],
        after=[combined],
    )
    return grad_tokens, grad_down.T[None]


def solution(mesh):
    token_spec = P(("dp", "expert"), None)
    weight_spec = P("expert", None, None)
    return jax.shard_map(
        on_device,
        mesh=mesh,
        in_specs=(token_spec,) * 5 + (weight_spec,) * 3,
        out_specs=(token_spec, P("expert", None, "dp")),
        check_vma=False,
    )
```
